32 devices in a mesh: expert: 16 (over z, y, core), narrow: 2 (over x).
Axes of the slice: x: 2, y: 2, z: 4, core: 2. Of those that a mesh axis runs over, the one named last changes fastest.
Arguments:
- tokens: bfloat16 [768, 4096], P('expert', 'narrow'), may hold values from -6 to 6
- route_ids: int32 [768, 8], P('expert'), may hold values from 0 to 15, all different within a row; in each aligned block of 48 rows (0 to 47, 48 to 95, ...) at most 48 rows name the same one
- route_weight: bfloat16 [768, 8], P('expert'), may hold values from 0.049804688 to 0.5
- partner: int32 [16], replicated, may hold values from 0 to 15, as said below
- old_place: int32 [16], replicated, may hold values from 0 to 15, each once
- gate_weight: bfloat16 [16, 768, 4096], P('expert', 'narrow'), may hold values from -0.09375 to 0.09375
- up_weight: bfloat16 [16, 768, 4096], P('expert', 'narrow'), may hold values from -0.09375 to 0.09375
- down_weight: bfloat16 [16, 768, 4096], P('expert', None, 'narrow'), may hold values from -0.21875 to 0.21875
Outputs:
- layer_out: bfloat16 [768, 4096], P('expert', 'narrow')
- new_gate: bfloat16 [16, 768, 4096], P('expert', 'narrow')
- new_up: bfloat16 [16, 768, 4096], P('expert', 'narrow')
- new_down: bfloat16 [16, 768, 4096], P('expert', None, 'narrow')
The draws below stay inside these ranges and needn't reach their ends.
Inputs may be any that keep to these rules, and one draw needn't show every extreme that they name: partner[partner[s]] == s for every slot; slots with partner[s] == s keep their weights; the number of pairs varies between draws from 1 to 8. `old_place`: a permutation of the experts. `route_ids`: each row names 8 different experts; among the 48 tokens of one index of expert, no expert is named by more than 48 tokens.
All inputs are finite; a program needn't handle non-finite values.
Results may differ from the reference program's by a relative error of at most 0.0058.
Values may be sent and summed in bfloat16 or wider, within the bound.
A program may use at most 128 MiB of HBM per device.

```python
import math
import jax
import jax.numpy as jnp
import numpy as np
from jax import lax

D = 4096
HID = 768
TOP = 8
TOK_GRP = 48
EXPERTS = 16
TOKENS = 768
CAP = 48
ROWS = 768


def draw_partner(key, part):
    order = jax.random.permutation(jax.random.fold_in(key, 11), EXPERTS).astype(jnp.int32)
    pairs = jax.random.randint(jax.random.fold_in(key, 12), (), 1, EXPERTS // 2 + 1)
    position = jnp.arange(EXPERTS, dtype=jnp.int32)
    mate = jnp.where(position < 2 * pairs, position + 1 - 2 * (position % 2), position)
    return jnp.zeros((EXPERTS,), jnp.int32).at[order].set(order[mate]).astype(jnp.int32)


def shard_levels(stream_key, extent, split, smallest, largest):
    gain = 1.0
    for axis_at, parts in split:
        heights = jax.random.uniform(jax.random.fold_in(jax.random.fold_in(stream_key, 6), axis_at), (parts,), jnp.float32, smallest / len(split), largest / len(split))
        gain = gain * jnp.repeat(jnp.exp(heights), extent[axis_at] // parts).reshape((-1,) + (1,) * (len(extent) - 1 - axis_at))
    return gain


def deal_out(stream_key, own, number, rows, amount, top, limit, lean):
    order = jax.random.permutation(stream_key, amount)
    crowded, common = load_shares(amount, rows * top, limit, lean, True), load_shares(amount, rows * top, limit, lean, False)
    places = jnp.arange(amount)

    def named(sizes, offset_by):
        used = int((sizes > 0).sum())
        fixed = max(1, used // 4)
        passed = fixed + (places - fixed + offset_by * (used - fixed)) % max(1, amount - fixed)
        return jnp.zeros((amount,), jnp.int32).at[order[jnp.where(places < fixed, places, passed)]].set(jnp.asarray(sizes, jnp.int32))

    sizes = jnp.where(number % 4 == 0, named(crowded, number // 4), named(common, number - number // 4 - 1))
    mixed = jax.random.permutation(jax.random.fold_in(own, 3), amount)
    giver, taker = mixed[0:amount // 2 * 2:2], mixed[1:amount // 2 * 2:2]
    room = jnp.minimum(sizes[giver] - 1, limit - sizes[taker]) // 2
    room = jnp.where((giver == order[0]) | (taker == order[0]) | (sizes[taker] == 0), 0, jnp.maximum(room, 0))
    passed = jax.random.randint(jax.random.fold_in(own, 4), (amount // 2,), 0, 1 << 20) % (room + 1)
    sizes = sizes.at[giver].add(-passed).at[taker].add(passed)
    labels = jnp.searchsorted(jnp.cumsum(sizes), jnp.arange(rows * top), side="right").astype(jnp.int32)
    table = labels.reshape(top, rows).T
    table = table[jax.random.permutation(jax.random.fold_in(own, 1), rows)]
    offset_by = jax.random.randint(jax.random.fold_in(own, 2), (rows, 1), 0, top)
    return jnp.take_along_axis(table, (jnp.arange(top)[None, :] + offset_by) % top, axis=1)


def load_shares(number_of, total, limit, slope, full):
    weights = [(1 << 20) // math.isqrt(standing ** slope) + 1 for standing in range(1, number_of + 1)]
    largest = limit if full else min(limit, max(-(-total // number_of), total * weights[0] // sum(weights)))
    least = 1 if total - largest >= number_of - 1 else 0
    counts, rest = [largest] + [least] * (number_of - 1), total - largest - least * (number_of - 1)
    while rest > 0:
        free = [i for i in range(1, number_of) if counts[i] < largest] or [i for i in range(1, number_of) if counts[i] < limit]
        pool, budget = sum([weights[i] for i in free]), rest
        for i in free:
            extra = min(limit - counts[i], max(1, budget * weights[i] // pool), rest)
            counts[i] = counts[i] + extra
            rest = rest - extra
    return np.array(counts)


def centred(stream_key, extent, scale, limit, shards=(), kind=jnp.bfloat16):
    gain = shard_levels(stream_key, extent, shards, -0.22, 0.18) if shards else 1.0
    result = jax.random.normal(stream_key, extent, jnp.float32) * scale * gain
    return jnp.minimum(jnp.maximum(result, -limit), limit).astype(kind)


def setup_inputs(seed: int = 0) -> dict:
    seeds = jax.random.split(jax.random.key(seed), 9)
    tokens = centred(seeds[0], (TOKENS, D), 1.0, 6.0, ((0, 16), (1, 2)))
    route_ids_keys = jax.random.split(jax.random.fold_in(seeds[1], 1), TOKENS // TOK_GRP)
    route_ids_turns = jax.random.permutation(jax.random.fold_in(seeds[1], 3), TOKENS // TOK_GRP)
    route_ids = jax.vmap(lambda own, number: deal_out(jax.random.fold_in(seeds[1], 2), own, number, TOK_GRP, EXPERTS, TOP, CAP, 2))(route_ids_keys, route_ids_turns).reshape((TOKENS, TOP))
    route_weight = jnp.clip(0.049804688 + 0.4501953 * jax.random.uniform(seeds[2], (TOKENS, TOP), jnp.float32) ** shard_levels(seeds[2], (TOKENS, TOP), ((0, 16),), -0.2, 0.2), 0.049804688, 0.5).astype(jnp.bfloat16)
    partner = draw_partner(jax.random.fold_in(seeds[8], 71), 0)
    old_place = jax.random.permutation(seeds[4], EXPERTS).astype(jnp.int32)
    gate_weight = centred(seeds[5], (EXPERTS, HID, D), D ** -0.5, 0.09375, ((0, 16), (1, 2)))
    up_weight = centred(seeds[6], (EXPERTS, HID, D), D ** -0.5, 0.09375, ((0, 16), (1, 2)))
    down_weight = centred(seeds[7], (EXPERTS, HID, D), HID ** -0.5, 0.21875, ((0, 16), (2, 2)))
    return dict(tokens=tokens, route_ids=route_ids, route_weight=route_weight, partner=partner, old_place=old_place, gate_weight=gate_weight, up_weight=up_weight, down_weight=down_weight)


def expert_block(rows_in, gate_slot, up_slot, down_slot):
    gate_sum = lax.dot_general(rows_in, gate_slot, (((1,), (1,)), ((), ())), preferred_element_type=jnp.float32)
    up_sum = lax.dot_general(rows_in, up_slot, (((1,), (1,)), ((), ())), preferred_element_type=jnp.float32)
    hidden = (jax.nn.silu(gate_sum) * up_sum).astype(jnp.bfloat16)
    return jnp.dot(hidden, down_slot, preferred_element_type=jnp.float32).astype(jnp.bfloat16)


def reference(tokens, route_ids, route_weight, partner, old_place, gate_weight, up_weight, down_weight):
    weights_full = route_weight.astype(jnp.float32)

    def per_slot(totals, inputs):
        gate_slot, up_slot, down_slot, expert_id = inputs
        chosen_mask = route_ids == expert_id
        chosen = jnp.any(chosen_mask, axis=1)
        share = jnp.sum(jnp.where(chosen_mask, weights_full, jnp.zeros_like(weights_full)), axis=1)
        position = (jnp.cumsum(chosen.astype(jnp.int32)) - 1).astype(jnp.int32)
        target = jnp.where(chosen, position, ROWS).astype(jnp.int32)
        buffer_rows = jnp.zeros((ROWS, D), jnp.bfloat16).at[target].set(tokens, mode="drop")
        produced = expert_block(buffer_rows, gate_slot, up_slot, down_slot)
        picked = jnp.take(produced, jnp.clip(position, 0, ROWS - 1).astype(jnp.int32), axis=0)
        return totals + share[:, None] * picked.astype(jnp.float32), None

    start_totals = jnp.zeros((TOKENS, D), jnp.float32)
    totals = lax.scan(per_slot, start_totals, (gate_weight, up_weight, down_weight, old_place))[0]
    new_gate = jnp.take(gate_weight, partner, axis=0)
    new_up = jnp.take(up_weight, partner, axis=0)
    new_down = jnp.take(down_weight, partner, axis=0)
    return (totals.astype(jnp.bfloat16), new_gate, new_up, new_down)
```

```python
import jax
import jax.numpy as jnp
from jax import lax
from jax.sharding import PartitionSpec as P


def contract_last(left, right):
    return lax.dot_general(
        left, right, (((1,), (1,)), ((), ())), preferred_element_type=jnp.float32
    )


def exchange_spread(partner, weights):
    groups = lax.axis_size("expert")

    def move(weight):
        pieces = weight.reshape(groups, -1)
        spread = lax.all_to_all(pieces, "expert", split_axis=0, concat_axis=0, tiled=True)
        ordered = jnp.take(spread, partner, axis=0)
        arrived = lax.all_to_all(ordered, "expert", split_axis=0, concat_axis=0, tiled=True)
        return arrived.reshape(weight.shape)

    return tuple(move(weight) for weight in weights)


def exchange(partner, weights):
    groups = lax.axis_size("expert")
    if groups > 16:
        return exchange_spread(partner, weights)
    me = lax.axis_index("expert")
    gate, up, down = (weight[0] for weight in weights)
    width = down.shape[1]
    pieces = [w[:, at : at + width] for w in (gate, up) for at in range(0, w.shape[1], width)]
    mine = jnp.concatenate(pieces + [down], axis=0)

    def swap(one, other):
        def run(held):
            taken = (me == one) | (me == other)
            moved = lax.ppermute(mine, "expert", [(one, other), (other, one)])
            return jnp.where(taken, moved, held)

        return run

    held = mine
    for one in range(groups - 1):
        others = range(one + 1, groups)
        held = lax.switch(
            jnp.maximum(partner[one] - one, 0),
            [lambda h: h] + [swap(one, other) for other in others],
            held,
        )
    rows, count = gate.shape[0], gate.shape[1] // width
    cut = [held[at * rows : (at + 1) * rows] for at in range(2 * count)]
    new_gate = jnp.concatenate(cut[:count], axis=1)
    new_up = jnp.concatenate(cut[count:], axis=1)
    return new_gate[None], new_up[None], held[2 * count * rows :][None]


def body(tokens, route_ids, route_weight, partner, old_place, gate_weight, up_weight, down_weight):
    groups = lax.axis_size("expert")
    halves = lax.axis_size("narrow")
    me = lax.axis_index("expert")
    rows, part = tokens.shape
    new_gate, new_up, new_down = exchange(partner, (gate_weight, up_weight, down_weight))

    matches = route_ids[:, :, None] == old_place[None, None, :]
    share = jnp.sum(jnp.where(matches, route_weight[:, :, None].astype(jnp.float32), 0.0), axis=1)
    share = jnp.pad(share.astype(jnp.bfloat16), ((0, 0), (0, -groups % 128)))
    packed = jnp.concatenate([tokens, share], axis=1)
    full = lax.all_gather(packed, ("expert", "narrow")).reshape(groups, halves, rows, -1)
    everything = jnp.swapaxes(full[..., :part], 1, 2).reshape(groups * rows, halves * part)
    shares = lax.dynamic_slice_in_dim(full[:, 0, :, part:], me, 1, axis=2).reshape(groups * rows, 1)

    gate_sum = contract_last(everything, gate_weight[0])
    up_sum = contract_last(everything, up_weight[0])
    hidden = (jax.nn.silu(gate_sum) * up_sum).astype(jnp.bfloat16)
    hidden = lax.all_gather(hidden, "narrow", axis=1, tiled=True)
    produced = jnp.dot(hidden, down_weight[0], preferred_element_type=jnp.float32)
    weighted = produced.astype(jnp.bfloat16).astype(jnp.float32) * shares.astype(jnp.float32)
    layer_out = lax.psum_scatter(
        weighted.astype(jnp.bfloat16), "expert", scatter_dimension=0, tiled=True
    )
    return (layer_out, new_gate, new_up, new_down)


def solution(mesh):
    return jax.shard_map(
        body,
        mesh=mesh,
        in_specs=(
            P("expert", "narrow"),
            P("expert", None),
            P("expert", None),
            P(),
            P(),
            P("expert", "narrow", None),
            P("expert", "narrow", None),
            P("expert", None, "narrow"),
        ),
        out_specs=(
            P("expert", "narrow"),
            P("expert", "narrow", None),
            P("expert", "narrow", None),
            P("expert", None, "narrow"),
        ),
        check_vma=False,
    )
```

```python
import jax
import jax.numpy as jnp
from jax import lax
from jax.sharding import PartitionSpec as P


def contract_last(left, right):
    return lax.dot_general(
        left, right, (((1,), (1,)), ((), ())), preferred_element_type=jnp.float32
    )


def exchange(partner, weights):
    groups = lax.axis_size("expert")

    def pieces_of(weight):
        rows, columns = weight.shape[1:]
        if rows % (8 * groups) == 0:
            return weight.reshape(groups, rows // groups, columns)
        return weight.reshape(groups, -1)

    spread = [
        lax.all_to_all(pieces_of(w), "expert", split_axis=0, concat_axis=0, tiled=True)
        for w in weights
    ]
    ordered = [jnp.take(s, partner, axis=0, mode="clip") for s in spread]
    arrived = [
        lax.all_to_all(o, "expert", split_axis=0, concat_axis=0, tiled=True) for o in ordered
    ]
    return tuple(a.reshape(w.shape) for a, w in zip(arrived, weights))


def body(tokens, route_ids, route_weight, partner, old_place, gate_weight, up_weight, down_weight):
    groups = lax.axis_size("expert")
    halves = lax.axis_size("narrow")
    me = lax.axis_index("expert")
    rows, part = tokens.shape
    new_gate, new_up, new_down = exchange(partner, (gate_weight, up_weight, down_weight))

    matches = route_ids[:, :, None] == old_place[None, None, :]
    share = jnp.sum(jnp.where(matches, route_weight[:, :, None].astype(jnp.float32), 0.0), axis=1)
    share = jnp.pad(share.astype(jnp.bfloat16), ((0, 0), (0, -groups % 128)))
    packed = jnp.concatenate([tokens, share], axis=1)
    full = lax.all_gather(packed, ("expert", "narrow")).reshape(groups, halves, rows, -1)
    everything = jnp.swapaxes(full[..., :part], 1, 2).reshape(groups * rows, halves * part)
    shares = lax.dynamic_slice_in_dim(full[:, 0, :, part:], me, 1, axis=2).reshape(groups * rows, 1)

    gate_sum = contract_last(everything, gate_weight[0])
    up_sum = contract_last(everything, up_weight[0])
    hidden = (jax.nn.silu(gate_sum) * up_sum).astype(jnp.bfloat16)
    hidden = lax.all_gather(hidden, "narrow", axis=1, tiled=True)
    produced = jnp.dot(hidden, down_weight[0], preferred_element_type=jnp.float32)
    weighted = produced.astype(jnp.bfloat16).astype(jnp.float32) * shares.astype(jnp.float32)
    layer_out = lax.psum_scatter(
        weighted.astype(jnp.bfloat16), "expert", scatter_dimension=0, tiled=True
    )
    return (layer_out, new_gate, new_up, new_down)


def solution(mesh):
    return jax.shard_map(
        body,
        mesh=mesh,
        in_specs=(
            P("expert", "narrow"),
            P("expert", None),
            P("expert", None),
            P(),
            P(),
            P("expert", "narrow", None),
            P("expert", "narrow", None),
            P("expert", None, "narrow"),
        ),
        out_specs=(
            P("expert", "narrow"),
            P("expert", "narrow", None),
            P("expert", "narrow", None),
            P("expert", None, "narrow"),
        ),
        check_vma=False,
    )
```

```python
import jax
import jax.numpy as jnp
from jax import lax
from jax.sharding import PartitionSpec as P


def contract_last(left, right):
    return lax.dot_general(
        left, right, (((1,), (1,)), ((), ())), preferred_element_type=jnp.float32
    )


def spread_out(partner, weights):
    groups = lax.axis_size("expert")

    def pieces_of(weight):
        rows, columns = weight.shape[1:]
        if rows % (8 * groups) == 0:
            return weight.reshape(groups, rows // groups, columns)
        return weight.reshape(groups, -1)

    spread = [
        lax.all_to_all(pieces_of(w), "expert", split_axis=0, concat_axis=0, tiled=True)
        for w in weights
    ]
    return [jnp.take(s, partner, axis=0, mode="clip") for s in spread]


def collect(ordered, weight):
    arrived = lax.all_to_all(ordered, "expert", split_axis=0, concat_axis=0, tiled=True)
    return arrived.reshape(weight.shape)


def body(tokens, route_ids, route_weight, partner, old_place, gate_weight, up_weight, down_weight):
    groups = lax.axis_size("expert")
    halves = lax.axis_size("narrow")
    me = lax.axis_index("expert")
    rows, part = tokens.shape
    gate_order, up_order, down_order = spread_out(partner, (gate_weight, up_weight, down_weight))

    matches = route_ids[:, :, None] == old_place[None, None, :]
    share = jnp.sum(jnp.where(matches, route_weight[:, :, None].astype(jnp.float32), 0.0), axis=1)
    share = jnp.pad(share.astype(jnp.bfloat16), ((0, 0), (0, -groups % 128)))
    packed = jnp.concatenate([tokens, share], axis=1)
    full = lax.all_gather(packed, ("expert", "narrow")).reshape(groups, halves, rows, -1)
    everything = jnp.swapaxes(full[..., :part], 1, 2).reshape(groups * rows, halves * part)
    shares = lax.dynamic_slice_in_dim(full[:, 0, :, part:], me, 1, axis=2).reshape(groups * rows, 1)

    gate_sum = contract_last(everything, gate_weight[0])
    up_sum = contract_last(everything, up_weight[0])
    hidden = (jax.nn.silu(gate_sum) * up_sum).astype(jnp.bfloat16)
    hidden, gate_order = lax.optimization_barrier((hidden, gate_order))
    new_gate = collect(gate_order, gate_weight)
    hidden = lax.all_gather(hidden, "narrow", axis=1, tiled=True)
    produced = jnp.dot(hidden, down_weight[0], preferred_element_type=jnp.float32)
    weighted = produced.astype(jnp.bfloat16).astype(jnp.float32) * shares.astype(jnp.float32)
    weighted, up_order, down_order = lax.optimization_barrier(
        (weighted.astype(jnp.bfloat16), up_order, down_order)
    )
    layer_out = lax.psum_scatter(weighted, "expert", scatter_dimension=0, tiled=True)
    new_up = collect(up_order, up_weight)
    new_down = collect(down_order, down_weight)
    return (layer_out, new_gate, new_up, new_down)


def solution(mesh):
    return jax.shard_map(
        body,
        mesh=mesh,
        in_specs=(
            P("expert", "narrow"),
            P("expert", None),
            P("expert", None),
            P(),
            P(),
            P("expert", "narrow", None),
            P("expert", "narrow", None),
            P("expert", None, "narrow"),
        ),
        out_specs=(
            P("expert", "narrow"),
            P("expert", "narrow", None),
            P("expert", "narrow", None),
            P("expert", None, "narrow"),
        ),
        check_vma=False,
    )
```
